256 devices in a mesh: rows: 128 (over z, y, x), rep: 2 (over core).
Axes of the slice: x: 4, y: 4, z: 8, core: 2. Of those that a mesh axis runs over, the one named last changes fastest.
Arguments:
- features: bfloat16 [32768, 128], P(('rows', 'rep')), may hold values from -6 to 6
- tile_counts: int32 [32768, 128, 128], P(('rows', 'rep')), may hold values from 0 to 3, as said below
- tile_row: int32 [32768], P(('rows', 'rep')), may hold values from 0 to 1
- tile_col: int32 [32768], P(('rows', 'rep')), may hold values from 0 to 255, as said below
- label_ids: int32 [16384], P(('rows', 'rep')), may hold values from 0 to 32767, as said below
- cotangent: bfloat16 [32768, 256], P(('rows', 'rep')), may hold values from -6 to 6
- self_weight: bfloat16 [128, 256], replicated, may hold values from -0.5 to 0.5
- neigh_weight: bfloat16 [128, 256], replicated, may hold values from -0.5 to 0.5
Outputs:
- activation: bfloat16 [32768, 256], P(('rows', 'rep'))
- grad_features: float32 [32768, 128], P(('rows', 'rep'))
- grad_self: float32 [128, 256], replicated
- grad_neigh: float32 [128, 256], replicated
The draws below stay inside these ranges and needn't reach their ends.
Inputs may be any that keep to these rules, and one draw needn't show every extreme that they name: `tile_counts`: edge counts of one tile; most entries are zero. `tile_col`: every tile held by a device of rep index c names a column block of the feature rows of some device of rep index c. On each device, at most 2 tiles name column blocks held by devices of one rows index, and exactly 2 do for some rows index. `label_ids`: the ids of one device's 64 labels are distinct and lie among that device's own feature rows.
All inputs are finite; a program needn't handle non-finite values.
Results may differ from the reference program's by a relative error of at most 0.0053.
Values may be sent and summed in bfloat16 or wider, within the bound.
No kernel may reach another device: no remote copies, remote signals or barrier semaphores. Data moves between devices by JAX's collectives and lax.ppermute only.
A program may use at most 128 MiB of HBM per device.

```python
import jax
import jax.numpy as jnp
from jax import lax

F_IN = 128
HID = 256
BLOCK = 128
NODES_DEV = 256
TILE_DEV = 128
HALF = 128
CAP = 2
LAB_DEV = 64
NODES = 32768
TILES = 32768
LABELS = 16384
N_ROWS = 128
N_REP = 2


def draw_tile_counts(key, part):
    present = jax.random.randint(key, (TILES, BLOCK, BLOCK), 0, 32, dtype=jnp.int32) == 0
    values = jax.random.randint(jax.random.fold_in(key, 1), (TILES, BLOCK, BLOCK), 1, 4, dtype=jnp.int32)
    return jnp.where(present, values, 0).astype(jnp.int32)


def draw_tile_col(key, part):
    per_half = HALF // BLOCK
    slot_total = CAP * N_ROWS

    def single(which):
        device_key = jax.random.fold_in(key, which)
        replica = which % N_REP
        owner_order = jax.random.permutation(jax.random.fold_in(device_key, 1), N_ROWS).astype(jnp.int32)
        slot_owner = owner_order[jnp.arange(slot_total, dtype=jnp.int32) // CAP]
        rest = jax.random.permutation(jax.random.fold_in(device_key, 2), slot_total - CAP).astype(jnp.int32)[:TILE_DEV - CAP] + CAP
        chosen = jnp.concatenate([jnp.arange(CAP, dtype=jnp.int32), rest])
        owners = slot_owner[chosen]
        shuffle = jax.random.permutation(jax.random.fold_in(device_key, 3), TILE_DEV).astype(jnp.int32)
        owners = owners[shuffle]
        within = jax.random.randint(jax.random.fold_in(device_key, 4), (TILE_DEV,), 0, per_half, dtype=jnp.int32)
        return ((owners * N_REP + replica) * per_half + within).astype(jnp.int32)
    return jax.vmap(single)(jnp.arange(N_ROWS * N_REP, dtype=jnp.int32)).reshape(-1).astype(jnp.int32)


def draw_label_ids(key, part):

    def single(which):
        shuffled = jax.random.permutation(jax.random.fold_in(key, which), HALF)
        return shuffled[:LAB_DEV].astype(jnp.int32) + which * HALF
    return jax.vmap(single)(jnp.arange(N_ROWS * N_REP, dtype=jnp.int32)).reshape(-1).astype(jnp.int32)


def place_ends(array, own_key, least, largest):
    spot = [jax.random.randint(jax.random.fold_in(own_key, axis), (), 0, length) for axis, length in enumerate(array.shape)]
    main_axis = array.shape.index(max(array.shape))
    beside = spot[:main_axis] + [(spot[main_axis] + 1) % array.shape[main_axis]] + spot[main_axis + 1:]
    return array.at[tuple(spot)].set(least).at[tuple(beside)].set(largest)


def levels(key, dims, split, smallest, largest):
    loudness, own = 1.0, jax.random.fold_in(key, 6)
    for position, blocks in split:
        draws = jnp.exp(jax.random.uniform(jax.random.fold_in(own, position), (blocks,), jnp.float32, smallest / len(split), largest / len(split)))
        loudness = loudness * jnp.repeat(draws, dims[position] // blocks).reshape([-1 if axis == position else 1 for axis in range(len(dims))])
    return loudness


def scatter_about(own_key, extent, scale, most, cuts=(), kind=jnp.bfloat16):
    array = scale * jax.random.normal(own_key, extent, jnp.float32)
    if cuts:
        array = array * levels(own_key, extent, cuts, -0.22, 0.18)
    return jnp.clip(array, -most, most).astype(kind)


def setup_inputs(seed: int = 0) -> dict:
    seeds = jax.random.split(jax.random.key(seed), 9)
    return {
        "features": scatter_about(seeds[0], (NODES, F_IN), 1.0, 6.0, ((0, 256),)),
        "tile_counts": draw_tile_counts(jax.random.fold_in(seeds[8], 71), 0),
        "tile_row": place_ends(jax.random.randint(seeds[2], (TILES,), 0, NODES_DEV // BLOCK), jax.random.fold_in(seeds[2], 1), 0, (NODES_DEV // BLOCK) - 1).astype(jnp.int32),
        "tile_col": draw_tile_col(jax.random.fold_in(seeds[8], 71), 0),
        "label_ids": draw_label_ids(jax.random.fold_in(seeds[8], 71), 0),
        "cotangent": scatter_about(seeds[5], (NODES, HID), 1.0, 6.0, ((0, 256),)),
        "self_weight": scatter_about(seeds[6], (F_IN, HID), F_IN ** -0.5, 0.5),
        "neigh_weight": scatter_about(seeds[7], (F_IN, HID), F_IN ** -0.5, 0.5),
    }


edge_moment = 14.0 / 96.0


def reference(features, tile_counts, tile_row, tile_col, label_ids, cotangent, self_weight, neigh_weight):
    row_blocks = NODES_DEV // BLOCK
    scale = (edge_moment * TILE_DEV * N_REP * BLOCK / row_blocks) ** -0.5
    group_tiles = TILE_DEV * N_REP
    counts = tile_counts.reshape(N_ROWS, group_tiles, BLOCK, BLOCK)
    rows_of = tile_row.reshape(N_ROWS, group_tiles)
    cols_of = tile_col.reshape(N_ROWS, group_tiles)
    feature_blocks = features.reshape(NODES // BLOCK, BLOCK, F_IN)

    def gather_group(inputs):
        count_part, row_part, col_part = inputs
        panels = feature_blocks[col_part].astype(jnp.float32)
        products = jnp.einsum('tij,tjf->tif', count_part.astype(jnp.float32), panels, precision=lax.Precision.HIGHEST)
        owner_table = (row_part[:, None] == jnp.arange(row_blocks, dtype=jnp.int32)[None, :]).astype(jnp.float32)
        return jnp.einsum('tr,tif->rif', owner_table, products, precision=lax.Precision.HIGHEST)

    summed = lax.map(gather_group, (counts, rows_of, cols_of)).reshape(NODES, F_IN)
    neighbour = (scale * summed).astype(jnp.bfloat16)
    preact = jnp.dot(features, self_weight, preferred_element_type=jnp.float32) + jnp.dot(neighbour, neigh_weight, preferred_element_type=jnp.float32)
    activation = jax.nn.silu(preact).astype(jnp.bfloat16)
    label_mask = jnp.zeros((NODES,), jnp.float32).at[label_ids].set(1.0)
    masked = cotangent.astype(jnp.float32) * label_mask[:, None]
    sigma = jax.nn.sigmoid(preact)
    delta = (masked * sigma * (1.0 + preact * (1.0 - sigma))).astype(jnp.bfloat16)
    grad_scale = float(LABELS) ** -0.5
    grad_self = grad_scale * jnp.einsum('nf,nh->fh', features.astype(jnp.float32), delta.astype(jnp.float32), precision=lax.Precision.HIGHEST)
    grad_neigh = grad_scale * jnp.einsum('nf,nh->fh', neighbour.astype(jnp.float32), delta.astype(jnp.float32), precision=lax.Precision.HIGHEST)
    back = jnp.einsum('nh,fh->nf', delta.astype(jnp.float32), neigh_weight.astype(jnp.float32), precision=lax.Precision.HIGHEST).astype(jnp.bfloat16)
    back_blocks = back.reshape(N_ROWS, row_blocks, BLOCK, F_IN)

    def spread(total, inputs):
        count_part, row_part, col_part, back_part = inputs
        picked = back_part[row_part].astype(jnp.float32)
        terms = jnp.einsum('tij,tif->tjf', count_part.astype(jnp.float32), picked, precision=lax.Precision.HIGHEST)
        rounded = lax.optimization_barrier(terms.astype(jnp.bfloat16))
        return total.at[col_part].add(rounded.astype(jnp.float32)), None

    start_total = jnp.zeros((NODES // BLOCK, BLOCK, F_IN), jnp.float32)
    total, unused = lax.scan(spread, start_total, (counts, rows_of, cols_of, back_blocks))
    own_term = jnp.einsum('nh,fh->nf', delta.astype(jnp.float32), self_weight.astype(jnp.float32), precision=lax.Precision.HIGHEST)
    grad_features = own_term + scale * total.reshape(NODES, F_IN)
    return (activation, grad_features, grad_self, grad_neigh)
```

```python
import functools

import jax
import jax.numpy as jnp
from jax import lax
from jax.experimental import pallas as pl
from jax.experimental.pallas import tpu as pltpu
from jax.sharding import Mesh
from jax.sharding import PartitionSpec as P

edge_moment = 14.0 / 96.0
f32, bf16 = jnp.float32, jnp.bfloat16
CHUNK = 16
ALL = ("z", "y", "x", "rep")
VMEM_LIMIT = 40 * 2**20


def params():
    return pltpu.CompilerParams(vmem_limit_bytes=VMEM_LIMIT)


def whole(shape):
    return pl.BlockSpec(shape, lambda *_: (0,) * len(shape))


def spread(block, axes):
    count = 1
    for axis in axes:
        count *= lax.axis_size(axis)
    copies = jnp.broadcast_to(block[None], (count,) + block.shape)
    return lax.all_to_all(copies, axes, 0, 0, tiled=True)


def gather_kernel(place_ref, slot_ref, counts_ref, features_ref, out_ref):
    step = pl.program_id(0)

    @pl.when(step == 0)
    def _():
        out_ref[...] = jnp.zeros_like(out_ref)

    for k in range(CHUNK):
        tile = step * CHUNK + k
        counts = counts_ref[k].astype(f32).astype(bf16)
        product = jnp.dot(counts, features_ref[place_ref[tile]], preferred_element_type=f32)
        out_ref[slot_ref[tile]] += product


def gather_products(place, slot, tile_counts, gathered):
    tiles, block, _ = tile_counts.shape
    return pl.pallas_call(
        gather_kernel,
        out_shape=jax.ShapeDtypeStruct((2, block, gathered.shape[-1]), f32),
        grid_spec=pltpu.PrefetchScalarGridSpec(
            num_scalar_prefetch=2,
            grid=(tiles // CHUNK,),
            in_specs=[
                pl.BlockSpec((CHUNK, block, block), lambda i, *_: (i, 0, 0)),
                whole(gathered.shape),
            ],
            out_specs=whole((2, block, gathered.shape[-1])),
        ),
        compiler_params=params(),
        cost_estimate=pl.CostEstimate(
            flops=2 * tiles * block**3, bytes_accessed=tile_counts.size * 4 + gathered.size * 2, transcendentals=0
        ),
        name="gather_products",
    )(place, slot, tile_counts, gathered)


def dense_kernel(
    scale,
    own_ref,
    other_ref,
    feat_ref,
    feat_other_ref,
    masked_ref,
    masked_other_ref,
    self_ref,
    neigh_ref,
    act_ref,
    back_ref,
    term_ref,
    grad_ref,
):
    contract_last = (((1,), (1,)), ((), ()))
    contract_first = (((0,), (0,)), ((), ()))
    for s, (feat_in, masked_in) in enumerate(((feat_ref, masked_ref), (feat_other_ref, masked_other_ref))):
        feat = feat_in[...]
        neighbour = (scale * (own_ref[s] + other_ref[1 - s])).astype(bf16)
        preact = jnp.dot(feat, self_ref[...], preferred_element_type=f32) + jnp.dot(
            neighbour, neigh_ref[...], preferred_element_type=f32
        )
        sigma = jax.nn.sigmoid(preact)
        delta = (masked_in[...].astype(f32) * sigma * (1.0 + preact * (1.0 - sigma))).astype(bf16)
        back_ref[s] = lax.dot_general(
            neigh_ref[...], delta, contract_last, preferred_element_type=f32
        ).astype(bf16)
        if s == 0:
            act_ref[...] = (preact * sigma).astype(bf16)
            term_ref[...] = lax.dot_general(self_ref[...], delta, contract_last, preferred_element_type=f32)
            grad_ref[0] = lax.dot_general(feat, delta, contract_first, preferred_element_type=f32)
            grad_ref[1] = lax.dot_general(neighbour, delta, contract_first, preferred_element_type=f32)


def spread_kernel(place_ref, slot_ref, counts_ref, back_ref, out_ref):
    step = pl.program_id(0)

    @pl.when(step == 0)
    def _():
        out_ref[...] = jnp.zeros_like(out_ref)

    for k in range(CHUNK):
        tile = step * CHUNK + k
        counts = counts_ref[k].astype(f32).astype(bf16)
        term = jnp.dot(back_ref[slot_ref[tile]], counts, preferred_element_type=f32).astype(bf16)
        place = place_ref[tile]
        out_ref[place] = (out_ref[place].astype(f32) + term.astype(f32)).astype(bf16)


def spread_terms(place, slot, tile_counts, back):
    tiles, block, _ = tile_counts.shape
    places = lax.axis_size("z") * lax.axis_size("y") * lax.axis_size("x")
    width = back.shape[1]
    return pl.pallas_call(
        spread_kernel,
        out_shape=jax.ShapeDtypeStruct((places, width, block), bf16),
        grid_spec=pltpu.PrefetchScalarGridSpec(
            num_scalar_prefetch=2,
            grid=(tiles // CHUNK,),
            in_specs=[
                pl.BlockSpec((CHUNK, block, block), lambda i, *_: (i, 0, 0)),
                whole(back.shape),
            ],
            out_specs=whole((places, width, block)),
        ),
        compiler_params=params(),
        cost_estimate=pl.CostEstimate(
            flops=2 * tiles * block**3, bytes_accessed=tile_counts.size * 4 + places * width * block * 2, transcendentals=0
        ),
        name="spread_terms",
    )(place, slot, tile_counts, back)


def middle_kernel(in_ref, out_ref):
    total = in_ref[0, 0].astype(f32)
    for k in range(1, in_ref.shape[0]):
        total += in_ref[k, 0].astype(f32)
    out_ref[0] = total.astype(bf16)


def middle_sum(parts):
    sources, kept, rows, columns = parts.shape
    return pl.pallas_call(
        middle_kernel,
        out_shape=jax.ShapeDtypeStruct((kept, rows, columns), bf16),
        grid=(kept,),
        in_specs=[pl.BlockSpec((sources, 1, rows, columns), lambda i: (0, i, 0, 0))],
        out_specs=pl.BlockSpec((1, rows, columns), lambda i: (i, 0, 0)),
        compiler_params=params(),
        name="middle_sum",
    )(parts)


def last_kernel(scale, in_ref, term_ref, out_ref):
    total = in_ref[0].astype(f32)
    for k in range(1, in_ref.shape[0]):
        total += in_ref[k].astype(f32)
    out_ref[...] = (term_ref[...] + scale * total).T


def shards(
    features, tile_counts, tile_row, tile_col, label_ids, cotangent, self_weight, neigh_weight
):
    half_rows, width_in = features.shape
    hidden = cotangent.shape[1]
    tile_total, block, _ = tile_counts.shape
    planes, ys, xs, reps = (lax.axis_size(a) for a in ALL)
    rep = lax.axis_index("rep")
    scale = (edge_moment * tile_total * reps * block / 2) ** (-0.5)
    swap = [(0, 1), (1, 0)]

    owner = tile_col // reps
    place = (owner % (ys * xs)) * planes + owner // (ys * xs)
    slot = jnp.bitwise_xor(tile_row, rep)

    near = spread(features, ("z",))
    gathered = spread(near.reshape(planes, half_rows, width_in), ("y", "x"))
    gathered = gathered.reshape(-1, half_rows, width_in)

    local_ids = label_ids % half_rows
    label_mask = jnp.any(local_ids[:, None] == jnp.arange(half_rows, dtype=jnp.int32)[None, :], axis=0)
    masked = jnp.where(label_mask[:, None], cotangent, jnp.zeros_like(cotangent))
    features_other = lax.ppermute(features, "rep", swap)
    masked_other = lax.ppermute(masked, "rep", swap)

    own = gather_products(place, slot, tile_counts, gathered)
    other = lax.ppermute(own, "rep", swap)

    activation, back, own_term, grads = pl.pallas_call(
        functools.partial(dense_kernel, scale),
        out_shape=(
            jax.ShapeDtypeStruct((half_rows, hidden), bf16),
            jax.ShapeDtypeStruct((2, width_in, half_rows), bf16),
            jax.ShapeDtypeStruct((width_in, half_rows), f32),
            jax.ShapeDtypeStruct((2, width_in, hidden), f32),
        ),
        compiler_params=params(),
        name="dense",
    )(own, other, features, features_other, masked, masked_other, self_weight, neigh_weight)

    terms = spread_terms(place, slot, tile_counts, back)
    first = lax.all_to_all(
        terms.reshape(ys * xs, planes, width_in, block), ("y", "x"), 0, 0, tiled=True
    )
    second = lax.all_to_all(middle_sum(first), ("z",), 0, 0, tiled=True)
    grad_features = pl.pallas_call(
        functools.partial(last_kernel, scale),
        out_shape=jax.ShapeDtypeStruct((half_rows, width_in), f32),
        compiler_params=params(),
        name="last_sum",
    )(second, own_term)

    cells = grads.reshape(ys * xs, -1, 128)
    cells = jnp.sum(lax.all_to_all(cells, ("y", "x"), 0, 0, tiled=True), axis=0)
    cells = jnp.sum(spread(cells, ("z", "rep")), axis=0)
    totals = spread(cells, ("y", "x")).reshape(2, width_in, hidden)
    grad_scale = float(label_ids.shape[0] * planes * ys * xs * reps) ** (-0.5)
    totals = grad_scale * totals
    return activation, grad_features, totals[0], totals[1]


def solution(mesh):
    grid = Mesh(mesh.devices.reshape(8, 4, 4, 2), ALL)
    placed = (
        P(ALL, None),
        P(ALL, None, None),
        P(ALL),
        P(ALL),
        P(ALL),
        P(ALL, None),
        P(),
        P(),
    )
    return jax.shard_map(
        shards,
        mesh=grid,
        in_specs=placed,
        out_specs=(P(ALL, None), P(ALL, None), P(), P()),
        check_vma=False,
    )
```

```python
import functools

import jax
import jax.numpy as jnp
from jax import lax
from jax.experimental import pallas as pl
from jax.experimental.pallas import tpu as pltpu
from jax.sharding import Mesh
from jax.sharding import PartitionSpec as P

edge_moment = 14.0 / 96.0
f32, bf16 = jnp.float32, jnp.bfloat16
CHUNK = 16
HIGH, LOW = ("zq", "yq", "xq"), ("zp", "yp", "xp", "rep")
ROWS = ("zq", "zp", "yq", "yp", "xq", "xp")
ALL = ROWS + ("rep",)
VMEM_LIMIT = 24 * 2**20
SMEM = pl.BlockSpec(memory_space=pltpu.SMEM)
VMEM = pl.BlockSpec(memory_space=pltpu.VMEM)
def params():
    return pltpu.CompilerParams(vmem_limit_bytes=VMEM_LIMIT)


def whole(shape):
    return pl.BlockSpec(shape, lambda *_: (0,) * len(shape))


def move(block, dz, dy, dx):
    pairs = [
        (z * 16 + y * 4 + x, (z + dz) % 8 * 16 + (y + dy) % 4 * 4 + (x + dx) % 4)
        for z in range(8)
        for y in range(4)
        for x in range(4)
    ]
    return lax.ppermute(block, ROWS, pairs)


def spread(block, axes):
    count = 1
    for axis in axes:
        count *= lax.axis_size(axis)
    copies = jnp.broadcast_to(block[None], (count,) + block.shape)
    return lax.all_to_all(copies, axes, 0, 0, tiled=True)


DETOUR = ((0, 0, 0), (0, 0, -1), (0, -1, 0), (2, 1, 1), (-1, 0, 0), (1, 2, 1), (1, 1, 2), (1, 1, 1))


def place_of(near, far):
    parity = jnp.bitwise_xor(near, far)
    parity = (parity >> 4 & 1) * 4 + (parity >> 2 & 1) * 2 + (parity & 1)
    extra = [sum(jnp.where(parity == c, step[k], 0) for c, step in enumerate(DETOUR)) for k in range(3)]
    z = ((far >> 4) - (near >> 4) + extra[0]) & 7
    y = ((far >> 2 & 3) - (near >> 2 & 3) + extra[1]) & 3
    x = ((far & 3) - (near & 3) + extra[2]) & 3
    return (parity * 16 + (y >> 1) * 8 + (x >> 1) * 4 + (z >> 1)).astype(jnp.int32)


def cast_kernel(in_ref, out_ref):
    out_ref[...] = in_ref[...].astype(f32).astype(bf16)


def cast_counts(tile_counts):
    tiles, block, _ = tile_counts.shape
    spec = pl.BlockSpec((CHUNK, block, block), lambda i: (i, 0, 0))
    return pl.pallas_call(
        cast_kernel,
        out_shape=jax.ShapeDtypeStruct(tile_counts.shape, bf16),
        grid=(tiles // CHUNK,),
        in_specs=[spec],
        out_specs=spec,
        compiler_params=params(),
        cost_estimate=pl.CostEstimate(flops=tile_counts.size, bytes_accessed=tile_counts.size * 6, transcendentals=0),
        name="cast_counts",
    )(tile_counts)


def gather_kernel(place_ref, slot_ref, counts_ref, *refs):
    parts, (out_ref, held_ref) = refs[:8], refs[8:]
    for k, part in enumerate(parts):
        held_ref[16 * k : 16 * k + 16] = part[...]
    out_ref[...] = jnp.zeros_like(out_ref)

    @pl.loop(0, counts_ref.shape[0] // CHUNK)
    def _(step):
        for k in range(CHUNK):
            tile = step * CHUNK + k
            product = jnp.dot(counts_ref[tile], held_ref[place_ref[tile]], preferred_element_type=f32)
            out_ref[slot_ref[tile]] += product


def gather_products(place, slot, counts, parts):
    tiles, block, _ = counts.shape
    width = parts[0].shape[-1]
    return pl.pallas_call(
        gather_kernel,
        out_shape=jax.ShapeDtypeStruct((2, block, width), f32),
        in_specs=[SMEM] * 2 + [VMEM] * 9,
        out_specs=VMEM,
        scratch_shapes=[pltpu.VMEM((128, block, width), bf16)],
        compiler_params=params(),
        cost_estimate=pl.CostEstimate(flops=2 * tiles * block**3, bytes_accessed=counts.size * 4, transcendentals=0),
        name="gather_products",
    )(place, slot, counts, *parts)


def dense_kernel(
    scale,
    own_ref,
    other_ref,
    feat_ref,
    feat_other_ref,
    masked_ref,
    masked_other_ref,
    self_ref,
    neigh_ref,
    act_ref,
    back_ref,
    term_ref,
    grad_ref,
):
    contract_last = (((1,), (1,)), ((), ()))
    contract_first = (((0,), (0,)), ((), ()))
    for s, (feat_in, masked_in) in enumerate(((feat_ref, masked_ref), (feat_other_ref, masked_other_ref))):
        feat = feat_in[...]
        neighbour = (scale * (own_ref[s] + other_ref[1 - s])).astype(bf16)
        preact = jnp.dot(feat, self_ref[...], preferred_element_type=f32) + jnp.dot(
            neighbour, neigh_ref[...], preferred_element_type=f32
        )
        sigma = jax.nn.sigmoid(preact)
        delta = (masked_in[...].astype(f32) * sigma * (1.0 + preact * (1.0 - sigma))).astype(bf16)
        back_ref[s] = lax.dot_general(
            neigh_ref[...], delta, contract_last, preferred_element_type=f32
        ).astype(bf16)
        if s == 0:
            act_ref[...] = (preact * sigma).astype(bf16)
            term_ref[...] = lax.dot_general(self_ref[...], delta, contract_last, preferred_element_type=f32)
            for k, value in enumerate((feat, neighbour)):
                grad = lax.dot_general(value, delta, contract_first, preferred_element_type=f32)
                grad_ref[2 * k], grad_ref[2 * k + 1] = grad[:, :128], grad[:, 128:]


def spread_kernel(place_ref, slot_ref, counts_ref, back_ref, *refs):
    outs, held_ref = refs[:8], refs[8]
    held_ref[...] = jnp.zeros_like(held_ref)

    @pl.loop(0, counts_ref.shape[0] // CHUNK)
    def _(step):
        for k in range(CHUNK):
            tile = step * CHUNK + k
            term = jnp.dot(back_ref[slot_ref[tile]], counts_ref[tile], preferred_element_type=f32).astype(bf16)
            place = place_ref[tile]
            held_ref[place] = (held_ref[place].astype(f32) + term.astype(f32)).astype(bf16)

    for k, out in enumerate(outs):
        out[...] = held_ref[16 * k : 16 * k + 16]


def spread_terms(place, slot, counts, back):
    tiles, block, _ = counts.shape
    width = back.shape[1]
    return pl.pallas_call(
        spread_kernel,
        out_shape=[jax.ShapeDtypeStruct((16, width, block), bf16)] * 8,
        in_specs=[SMEM] * 2 + [VMEM] * 2,
        out_specs=[VMEM] * 8,
        scratch_shapes=[pltpu.VMEM((128, width, block), bf16)],
        compiler_params=params(),
        cost_estimate=pl.CostEstimate(flops=2 * tiles * block**3, bytes_accessed=counts.size * 4, transcendentals=0),
        name="spread_terms",
    )(place, slot, counts, back)


def add_up(refs, index):
    total = refs[0][index].astype(f32)
    for ref in refs[1:]:
        total += ref[index].astype(f32)
    return total


def class_kernel(*refs):
    @pl.loop(0, refs[0].shape[0])
    def _(k):
        refs[-1][k] = add_up(refs[:-1], k).astype(bf16)


def class_sum(parts):
    return pl.pallas_call(
        class_kernel,
        out_shape=jax.ShapeDtypeStruct(parts[0].shape, bf16),
        in_specs=[VMEM] * len(parts),
        out_specs=VMEM,
        compiler_params=params(),
        name="class_sum",
    )(*parts)


def joint_kernel(cells_ref, *refs):
    ins, outs = refs[:5], refs[5:]
    rows = ins[0].shape[1]
    for k, out in enumerate(outs):
        for z in range(4):
            out[z * rows : z * rows + rows] = add_up(ins, 4 * k + z).astype(bf16)
        out[4 * rows :] = cells_ref[...].astype(bf16)


def joint_sum(cells, parts):
    _, rows, columns = parts[0].shape
    return pl.pallas_call(
        joint_kernel,
        out_shape=[jax.ShapeDtypeStruct((4 * rows + cells.shape[0], columns), bf16)] * 4,
        in_specs=[VMEM] * 6,
        out_specs=[VMEM] * 4,
        compiler_params=params(),
        name="joint_sum",
    )(cells, *parts)


def plane_kernel(*refs):
    ins, outs = refs[:4], refs[4:]
    rows = 128
    for z, out in enumerate(outs):
        out[:rows] = add_up(ins, slice(z * rows, z * rows + rows)).astype(bf16)
        for k, part in enumerate(ins):
            out[rows + 32 * k : rows + 32 * k + 32] = part[4 * rows :]


def plane_sum(parts):
    columns = parts[0].shape[1]
    return pl.pallas_call(
        plane_kernel,
        out_shape=[jax.ShapeDtypeStruct((256, columns), bf16)] * 4,
        in_specs=[VMEM] * 4,
        out_specs=[VMEM] * 4,
        compiler_params=params(),
        name="plane_sum",
    )(*parts)


def last_kernel(scale, grad_scale, order_ref, *refs):
    ins, (term_ref, out_ref, self_ref, neigh_ref, cells_ref) = refs[:4], refs[4:]
    rows = term_ref.shape[0]
    total = add_up(ins, slice(0, rows))
    out_ref[...] = (term_ref[...] + scale * total).T
    for z, part in enumerate(ins):
        for k in range(4):
            cells = part[rows + 32 * k : rows + 32 * k + 32].astype(f32)
            cells_ref[order_ref[4 * k + z]] = grad_scale * cells
    for k in range(16):
        ref = (self_ref, neigh_ref)[k // 8]
        ref[k % 4 * 32 : k % 4 * 32 + 32, k // 4 % 2 * 128 : k // 4 % 2 * 128 + 128] = cells_ref[k]


def gather_blocks(features, tile_counts):
    own = features[None]
    own = jnp.concatenate([own, move(own, 2, 0, 0), move(own, 4, 0, 0), move(own, -2, 0, 0)])
    own = jnp.concatenate([own, move(own, 0, 0, 2), move(own, 0, 2, 0), move(own, 0, 2, 2)])
    own, tile_counts = lax.optimization_barrier((own, tile_counts))
    far = move(own, -1, -1, -1)
    by_x, by_y, by_z = move(own, 0, 0, 1), move(own, 0, 1, 0), move(own, 1, 0, 0)
    parts = [own, by_x, by_y, move(far, -1, 0, 0), by_z, move(far, 0, -1, 0), move(far, 0, 0, -1), far]
    return parts, tile_counts


def reduce_blocks(terms):
    far = class_sum([terms[7], move(terms[6], 0, 0, -1), move(terms[5], 0, -1, 0), move(terms[3], -1, 0, 0)])
    direct = [move(terms[1], 0, 0, 1), move(terms[2], 0, 1, 0), move(terms[4], 1, 0, 0)]
    return [terms[0], *direct, move(far, -1, -1, -1)]


def shards(
    features, tile_counts, tile_row, tile_col, label_ids, cotangent, self_weight, neigh_weight
):
    half_rows, width_in = features.shape
    hidden = cotangent.shape[1]
    tile_total, block, _ = tile_counts.shape
    reps, devices = lax.axis_size("rep"), lax.axis_size(ALL)
    rep = lax.axis_index("rep")
    scale = (edge_moment * tile_total * reps * block / 2) ** (-0.5)
    swap = [(0, 1), (1, 0)]

    owner, here = tile_col // reps, lax.axis_index(ROWS)
    source, target = place_of(owner, here), place_of(here, owner)
    step = jnp.arange(16, dtype=jnp.int32)
    order = (here // 32 - step % 4) % 4 * 4 + (here // 8 + step // 8) % 2 * 2 + (here // 2 + step // 4) % 2
    slot = jnp.bitwise_xor(tile_row, rep)

    gathered, tile_counts = gather_blocks(features, tile_counts)
    counts = cast_counts(tile_counts)

    local_ids = label_ids % half_rows
    label_mask = jnp.any(local_ids[:, None] == jnp.arange(half_rows, dtype=jnp.int32)[None, :], axis=0)
    masked = jnp.where(label_mask[:, None], cotangent, jnp.zeros_like(cotangent))
    features_other = lax.ppermute(features, "rep", swap)
    masked_other = lax.ppermute(masked, "rep", swap)

    own = gather_products(source, slot, counts, gathered)
    other = lax.ppermute(own, "rep", swap)

    activation, back, own_term, grads = pl.pallas_call(
        functools.partial(dense_kernel, scale),
        out_shape=(
            jax.ShapeDtypeStruct((half_rows, hidden), bf16),
            jax.ShapeDtypeStruct((2, width_in, half_rows), bf16),
            jax.ShapeDtypeStruct((width_in, half_rows), f32),
            jax.ShapeDtypeStruct((4, width_in, 128), f32),
        ),
        compiler_params=params(),
        name="dense",
    )(own, other, features, features_other, masked, masked_other, self_weight, neigh_weight)

    terms = spread_terms(target, slot, counts, back)
    *terms, grads = lax.optimization_barrier((*terms, grads))
    parts = reduce_blocks(terms)

    cells = grads.reshape(lax.axis_size(HIGH), -1, 128)
    cells = jnp.sum(lax.all_to_all(cells, HIGH, 0, 0, tiled=True), axis=0)
    cells = jnp.sum(spread(cells, LOW), axis=0)
    parts = joint_sum(cells, parts)
    parts = plane_sum([parts[0], move(parts[1], 0, 0, 2), move(parts[2], 0, 2, 0), move(parts[3], 0, 2, 2)])
    parts = [parts[0], move(parts[1], 2, 0, 0), move(parts[2], 4, 0, 0), move(parts[3], -2, 0, 0)]
    grad_scale = float(label_ids.shape[0] * devices) ** (-0.5)
    grad_shape = jax.ShapeDtypeStruct((width_in, hidden), f32)
    grad_features, grad_self, grad_neigh = pl.pallas_call(
        functools.partial(last_kernel, scale, grad_scale),
        out_shape=(jax.ShapeDtypeStruct((half_rows, width_in), f32), grad_shape, grad_shape),
        in_specs=[SMEM] + [VMEM] * 5,
        out_specs=(VMEM, VMEM, VMEM),
        scratch_shapes=[pltpu.VMEM((16, 32, 128), f32)],
        compiler_params=params(),
        name="last_sum",
    )(order, *parts, own_term)
    return activation, grad_features, grad_self, grad_neigh


def solution(mesh):
    grid = Mesh(mesh.devices.reshape(4, 2, 2, 2, 2, 2, 2), ALL)
    placed = (
        P(ALL, None),
        P(ALL, None, None),
        P(ALL),
        P(ALL),
        P(ALL),
        P(ALL, None),
        P(),
        P(),
    )
    return jax.shard_map(
        shards,
        mesh=grid,
        in_specs=placed,
        out_specs=(P(ALL, None), P(ALL, None), P(), P()),
        check_vma=False,
    )
```

```python
import functools

import jax
import jax.numpy as jnp
from jax import lax
from jax.experimental import pallas as pl
from jax.experimental.pallas import tpu as pltpu
from jax.sharding import Mesh
from jax.sharding import PartitionSpec as P

edge_moment = 14.0 / 96.0
f32, bf16 = jnp.float32, jnp.bfloat16
CHUNK = 16
UNROLL = 8
NEAR, FAR = (0, 1, 2, 4, 7), (3, 5, 6)
HIGH, LOW = ("zq", "yq", "xq"), ("zp", "yp", "xp", "rep")
ROWS = ("zq", "zp", "yq", "yp", "xq", "xp")
ALL = ROWS + ("rep",)
VMEM_LIMIT = 16 * 2**20
SMEM = pl.BlockSpec(memory_space=pltpu.SMEM)
VMEM = pl.BlockSpec(memory_space=pltpu.VMEM)
def params():
    return pltpu.CompilerParams(vmem_limit_bytes=VMEM_LIMIT)


def whole(shape):
    return pl.BlockSpec(shape, lambda *_: (0,) * len(shape))


def move(block, dz, dy, dx):
    pairs = [
        (z * 16 + y * 4 + x, (z + dz) % 8 * 16 + (y + dy) % 4 * 4 + (x + dx) % 4)
        for z in range(8)
        for y in range(4)
        for x in range(4)
    ]
    return lax.ppermute(block, ROWS, pairs)


def spread(block, axes):
    count = 1
    for axis in axes:
        count *= lax.axis_size(axis)
    copies = jnp.broadcast_to(block[None], (count,) + block.shape)
    return lax.all_to_all(copies, axes, 0, 0, tiled=True)


DETOUR = ((0, 0, 0), (0, 0, -1), (0, -1, 0), (2, 1, 1), (-1, 0, 0), (1, 2, 1), (1, 1, 2), (1, 1, 1))


def place_of(near, far):
    parity = jnp.bitwise_xor(near, far)
    parity = (parity >> 4 & 1) * 4 + (parity >> 2 & 1) * 2 + (parity & 1)
    extra = [sum(jnp.where(parity == c, step[k], 0) for c, step in enumerate(DETOUR)) for k in range(3)]
    z = ((far >> 4) - (near >> 4) + extra[0]) & 7
    y = ((far >> 2 & 3) - (near >> 2 & 3) + extra[1]) & 3
    x = ((far & 3) - (near & 3) + extra[2]) & 3
    return (parity * 16 + (y >> 1) * 8 + (x >> 1) * 4 + (z >> 1)).astype(jnp.int32)


def cast_kernel(in_ref, out_ref):
    out_ref[...] = in_ref[...].astype(jnp.int8)


def cast_counts(tile_counts):
    tiles, block, _ = tile_counts.shape
    spec = pl.BlockSpec((CHUNK, block, block), lambda i: (i, 0, 0))
    return pl.pallas_call(
        cast_kernel,
        out_shape=jax.ShapeDtypeStruct(tile_counts.shape, jnp.int8),
        grid=(tiles // CHUNK,),
        in_specs=[spec],
        out_specs=spec,
        compiler_params=params(),
        cost_estimate=pl.CostEstimate(flops=tile_counts.size, bytes_accessed=tile_counts.size * 5, transcendentals=0),
        name="cast_counts",
    )(tile_counts)


def for_tiles(far, rounds_ref, work_ref, body):
    start, stop = (rounds_ref[0], rounds_ref[1]) if far else (0, rounds_ref[0])

    def several(step, carry):
        for k in range(UNROLL):
            work = work_ref[step * UNROLL + k]
            body(work & 127, work >> 7 & 255, work >> 15 & 255, work >> 23)
        return carry

    lax.fori_loop(start, stop, several, 0)


def gather_kernel(far, rounds_ref, work_ref, counts_ref, *refs):
    codes = FAR if far else NEAR
    parts, (out_ref, held_ref) = refs[: len(codes)], refs[-2:]
    for code, part in zip(codes, parts):
        held_ref[16 * code : 16 * code + 16] = part[...]
    held_ref[128] = jnp.zeros_like(held_ref[128])
    out_ref[...] = refs[len(codes)][...] if far else jnp.zeros_like(out_ref)

    def body(tile, source, target, slot):
        out_ref[slot] += jnp.dot(counts_ref[tile].astype(f32).astype(bf16), held_ref[source], preferred_element_type=f32)

    for_tiles(far, rounds_ref, work_ref, body)


def gather_products(far, rounds, work, counts, parts, *before):
    tiles, block, _ = counts.shape
    width = parts[0].shape[-1]
    return pl.pallas_call(
        functools.partial(gather_kernel, far),
        out_shape=jax.ShapeDtypeStruct((2, block, width), f32),
        in_specs=[SMEM] * 2 + [VMEM] * (1 + len(parts) + len(before)),
        out_specs=VMEM,
        scratch_shapes=[pltpu.VMEM((129, block, width), bf16)],
        compiler_params=params(),
        cost_estimate=pl.CostEstimate(flops=2 * tiles * block**3, bytes_accessed=counts.size * 2, transcendentals=0),
        name="far_products" if far else "near_products",
    )(rounds, work, counts, *parts, *before)


def dense_kernel(
    scale,
    own_ref,
    other_ref,
    feat_ref,
    feat_other_ref,
    masked_ref,
    masked_other_ref,
    self_ref,
    neigh_ref,
    act_ref,
    back_ref,
    term_ref,
    grad_ref,
):
    contract_last = (((1,), (1,)), ((), ()))
    contract_first = (((0,), (0,)), ((), ()))
    for s, (feat_in, masked_in) in enumerate(((feat_ref, masked_ref), (feat_other_ref, masked_other_ref))):
        feat = feat_in[...]
        neighbour = (scale * (own_ref[s] + other_ref[1 - s])).astype(bf16)
        preact = jnp.dot(feat, self_ref[...], preferred_element_type=f32) + jnp.dot(
            neighbour, neigh_ref[...], preferred_element_type=f32
        )
        sigma = jax.nn.sigmoid(preact)
        delta = (masked_in[...].astype(f32) * sigma * (1.0 + preact * (1.0 - sigma))).astype(bf16)
        back_ref[s] = lax.dot_general(
            neigh_ref[...], delta, contract_last, preferred_element_type=f32
        ).astype(bf16)
        if s == 0:
            act_ref[...] = (preact * sigma).astype(bf16)
            term_ref[...] = lax.dot_general(self_ref[...], delta, contract_last, preferred_element_type=f32)
            for k, value in enumerate((feat, neighbour)):
                grad = lax.dot_general(value, delta, contract_first, preferred_element_type=f32)
                grad_ref[2 * k], grad_ref[2 * k + 1] = grad[:, :128], grad[:, 128:]


def spread_kernel(far, rounds_ref, work_ref, counts_ref, back_ref, *refs):
    codes = FAR if far else NEAR
    outs, held_ref = refs[:-1], refs[-1]
    for code in codes:
        held_ref[16 * code : 16 * code + 16] = jnp.zeros_like(outs[0])
    held_ref[128] = jnp.zeros_like(held_ref[128])

    def body(tile, source, target, slot):
        term = jnp.dot(back_ref[slot], counts_ref[tile].astype(f32).astype(bf16), preferred_element_type=f32).astype(bf16)
        held_ref[target] = (held_ref[target].astype(f32) + term.astype(f32)).astype(bf16)

    for_tiles(far, rounds_ref, work_ref, body)
    for code, out in zip(codes, outs):
        out[...] = held_ref[16 * code : 16 * code + 16]


def spread_terms(far, rounds, work, counts, back):
    tiles, block, _ = counts.shape
    width = back.shape[1]
    outs = len(FAR if far else NEAR)
    return pl.pallas_call(
        functools.partial(spread_kernel, far),
        out_shape=[jax.ShapeDtypeStruct((16, width, block), bf16)] * outs,
        in_specs=[SMEM] * 2 + [VMEM] * 2,
        out_specs=[VMEM] * outs,
        scratch_shapes=[pltpu.VMEM((129, width, block), bf16)],
        compiler_params=params(),
        cost_estimate=pl.CostEstimate(flops=2 * tiles * block**3, bytes_accessed=counts.size * 2, transcendentals=0),
        name="far_terms" if far else "near_terms",
    )(rounds, work, counts, back)


def add_up(refs, index):
    total = refs[0][index].astype(f32)
    for ref in refs[1:]:
        total += ref[index].astype(f32)
    return total


def class_kernel(*refs):
    @pl.loop(0, refs[0].shape[0])
    def _(k):
        refs[-1][k] = add_up(refs[:-1], k).astype(bf16)


def class_sum(parts):
    return pl.pallas_call(
        class_kernel,
        out_shape=jax.ShapeDtypeStruct(parts[0].shape, bf16),
        in_specs=[VMEM] * len(parts),
        out_specs=VMEM,
        compiler_params=params(),
        name="class_sum",
    )(*parts)


def joint_kernel(cells_ref, *refs):
    ins, outs = refs[:5], refs[5:]
    rows = ins[0].shape[1]
    for k, out in enumerate(outs):
        for z in range(4):
            out[z * rows : z * rows + rows] = add_up(ins, 4 * k + z).astype(bf16)
        out[4 * rows :] = cells_ref[...].astype(bf16)


def joint_sum(cells, parts):
    _, rows, columns = parts[0].shape
    return pl.pallas_call(
        joint_kernel,
        out_shape=[jax.ShapeDtypeStruct((4 * rows + cells.shape[0], columns), bf16)] * 4,
        in_specs=[VMEM] * 6,
        out_specs=[VMEM] * 4,
        compiler_params=params(),
        name="joint_sum",
    )(cells, *parts)


def plane_kernel(*refs):
    ins, outs = refs[:4], refs[4:]
    rows = 128
    for z, out in enumerate(outs):
        out[:rows] = add_up(ins, slice(z * rows, z * rows + rows)).astype(bf16)
        for k, part in enumerate(ins):
            out[rows + 32 * k : rows + 32 * k + 32] = part[4 * rows :]


def plane_sum(parts):
    columns = parts[0].shape[1]
    return pl.pallas_call(
        plane_kernel,
        out_shape=[jax.ShapeDtypeStruct((256, columns), bf16)] * 4,
        in_specs=[VMEM] * 4,
        out_specs=[VMEM] * 4,
        compiler_params=params(),
        name="plane_sum",
    )(*parts)


def last_kernel(scale, grad_scale, order_ref, *refs):
    ins, (term_ref, out_ref, self_ref, neigh_ref, cells_ref) = refs[:4], refs[4:]
    rows = term_ref.shape[0]
    total = add_up(ins, slice(0, rows))
    out_ref[...] = (term_ref[...] + scale * total).T
    for z, part in enumerate(ins):
        for k in range(4):
            cells = part[rows + 32 * k : rows + 32 * k + 32].astype(f32)
            cells_ref[order_ref[4 * k + z]] = grad_scale * cells
    for k in range(16):
        ref = (self_ref, neigh_ref)[k // 8]
        ref[k % 4 * 32 : k % 4 * 32 + 32, k // 4 % 2 * 128 : k // 4 % 2 * 128 + 128] = cells_ref[k]


def gather_blocks(features, tile_counts, *ready):
    own = features[None]
    own = jnp.concatenate([own, move(own, 2, 0, 0), move(own, 4, 0, 0), move(own, -2, 0, 0)])
    own = jnp.concatenate([own, move(own, 0, 0, 2), move(own, 0, 2, 0), move(own, 0, 2, 2)])
    own, tile_counts = lax.optimization_barrier((own, tile_counts))
    far = move(own, -1, -1, -1)
    counts = cast_counts(tile_counts)
    far, counts, *ready = lax.optimization_barrier((far, counts, *ready))
    near = [own, move(own, 0, 0, 1), move(own, 0, 1, 0), move(own, 1, 0, 0), far]
    return near, [move(far, -1, 0, 0), move(far, 0, -1, 0), move(far, 0, 0, -1)], counts, *ready


def shards(
    features, tile_counts, tile_row, tile_col, label_ids, cotangent, self_weight, neigh_weight
):
    half_rows, width_in = features.shape
    hidden = cotangent.shape[1]
    tile_total, block, _ = tile_counts.shape
    reps, devices = lax.axis_size("rep"), lax.axis_size(ALL)
    rep = lax.axis_index("rep")
    scale = (edge_moment * tile_total * reps * block / 2) ** (-0.5)
    swap = [(0, 1), (1, 0)]

    owner, here = tile_col >> 1, lax.axis_index(ROWS)
    source, target = place_of(owner, here), place_of(here, owner)
    step = jnp.arange(16, dtype=jnp.int32)
    order = ((here >> 5) - step & 3) * 4 + ((here >> 3) + (step >> 3) & 1) * 2 + ((here >> 1) + (step >> 2) & 1)
    slot = jnp.bitwise_xor(tile_row, rep)
    tiles = jnp.arange(tile_total, dtype=jnp.int32)
    near_tile = functools.reduce(jnp.logical_and, [source // 16 != code for code in FAR])
    before = tiles[None, :] < tiles[:, None]
    rank = jnp.sum(before & (near_tile[None, :] == near_tile[:, None]), axis=1, dtype=jnp.int32)
    near_rounds = jnp.sum(near_tile, dtype=jnp.int32) + UNROLL - 1 >> 3
    far_rounds = jnp.sum(~near_tile, dtype=jnp.int32) + UNROLL - 1 >> 3
    rounds = jnp.stack([near_rounds, near_rounds + far_rounds])
    rank = jnp.where(near_tile, rank, near_rounds * UNROLL + rank)
    unused = 128 * 2**7 + 128 * 2**15
    work = tiles + source * 2**7 + target * 2**15 + slot * 2**23 - unused
    entries = jnp.arange(tile_total + 2 * UNROLL, dtype=jnp.int32)
    work = unused + jnp.sum(jnp.where(rank[None, :] == entries[:, None], work[None, :], 0), axis=1, dtype=jnp.int32)

    local_ids = label_ids % half_rows
    label_mask = jnp.any(local_ids[:, None] == jnp.arange(half_rows, dtype=jnp.int32)[None, :], axis=0)
    masked = jnp.where(label_mask[:, None], cotangent, jnp.zeros_like(cotangent))
    near, far, counts, rounds, work, masked = gather_blocks(features, tile_counts, rounds, work, masked)
    features_other = lax.ppermute(features, "rep", swap)
    masked_other = lax.ppermute(masked, "rep", swap)

    own = gather_products(False, rounds, work, counts, near)
    own, features_other, masked_other = lax.optimization_barrier((own, features_other, masked_other))
    own = gather_products(True, rounds, work, counts, far, own)
    other = lax.ppermute(own, "rep", swap)

    activation, back, own_term, grads = pl.pallas_call(
        functools.partial(dense_kernel, scale),
        out_shape=(
            jax.ShapeDtypeStruct((half_rows, hidden), bf16),
            jax.ShapeDtypeStruct((2, width_in, half_rows), bf16),
            jax.ShapeDtypeStruct((width_in, half_rows), f32),
            jax.ShapeDtypeStruct((4, width_in, 128), f32),
        ),
        compiler_params=params(),
        name="dense",
    )(own, other, features, features_other, masked, masked_other, self_weight, neigh_weight)

    far = spread_terms(True, rounds, work, counts, back)
    *far, grads = lax.optimization_barrier((*far, grads))
    far = [move(far[0], -1, 0, 0), move(far[1], 0, -1, 0), move(far[2], 0, 0, -1)]
    near = spread_terms(False, rounds, work, counts, back)
    parts = [near[0], move(near[1], 0, 0, 1), move(near[2], 0, 1, 0), move(near[3], 1, 0, 0)]
    parts.append(move(class_sum([near[4], *far]), -1, -1, -1))

    cells = grads.reshape(lax.axis_size(HIGH), -1, 128)
    cells = jnp.sum(lax.all_to_all(cells, HIGH, 0, 0, tiled=True), axis=0)
    cells = jnp.sum(spread(cells, LOW), axis=0)
    parts = joint_sum(cells, parts)
    parts = plane_sum([parts[0], move(parts[1], 0, 0, 2), move(parts[2], 0, 2, 0), move(parts[3], 0, 2, 2)])
    parts = [parts[0], move(parts[1], 2, 0, 0), move(parts[2], 4, 0, 0), move(parts[3], -2, 0, 0)]
    grad_scale = float(label_ids.shape[0] * devices) ** (-0.5)
    grad_shape = jax.ShapeDtypeStruct((width_in, hidden), f32)
    grad_features, grad_self, grad_neigh = pl.pallas_call(
        functools.partial(last_kernel, scale, grad_scale),
        out_shape=(jax.ShapeDtypeStruct((half_rows, width_in), f32), grad_shape, grad_shape),
        in_specs=[SMEM] + [VMEM] * 5,
        out_specs=(VMEM, VMEM, VMEM),
        scratch_shapes=[pltpu.VMEM((16, 32, 128), f32)],
        compiler_params=params(),
        name="last_sum",
    )(order, *parts, own_term)
    return activation, grad_features, grad_self, grad_neigh


def solution(mesh):
    grid = Mesh(mesh.devices.reshape(4, 2, 2, 2, 2, 2, 2), ALL)
    placed = (
        P(ALL, None),
        P(ALL, None, None),
        P(ALL),
        P(ALL),
        P(ALL),
        P(ALL, None),
        P(),
        P(),
    )
    return jax.shard_map(
        shards,
        mesh=grid,
        in_specs=placed,
        out_specs=(P(ALL, None), P(ALL, None), P(), P()),
        check_vma=False,
    )
```

```python
import functools

import jax
import jax.numpy as jnp
from jax import lax
from jax.experimental import pallas as pl
from jax.experimental.pallas import tpu as pltpu
from jax.sharding import Mesh
from jax.sharding import PartitionSpec as P

edge_moment = 14.0 / 96.0
f32, bf16 = jnp.float32, jnp.bfloat16
CHUNK = 16
UNROLL = 8
NEAR, FAR = (0, 1, 2, 4, 7), (3, 5, 6)
HIGH, LOW = ("zq", "yq", "xq"), ("zp", "yp", "xp")
ROWS = ("zq", "zp", "yq", "yp", "xq", "xp")
ALL = ROWS + ("rep",)
VMEM_LIMIT = 16 * 2**20
SMEM = pl.BlockSpec(memory_space=pltpu.SMEM)
VMEM = pl.BlockSpec(memory_space=pltpu.VMEM)
def params():
    return pltpu.CompilerParams(vmem_limit_bytes=VMEM_LIMIT)


def whole(shape):
    return pl.BlockSpec(shape, lambda *_: (0,) * len(shape))


def move(block, dz, dy, dx):
    pairs = [
        (z * 16 + y * 4 + x, (z + dz) % 8 * 16 + (y + dy) % 4 * 4 + (x + dx) % 4)
        for z in range(8)
        for y in range(4)
        for x in range(4)
    ]
    return lax.ppermute(block, ROWS, pairs)


def spread(block, axes):
    count = 1
    for axis in axes:
        count *= lax.axis_size(axis)
    copies = jnp.broadcast_to(block[None], (count,) + block.shape)
    return lax.all_to_all(copies, axes, 0, 0, tiled=True)


DETOUR = ((0, 0, 0), (0, 0, -1), (0, -1, 0), (2, 1, 1), (-1, 0, 0), (1, 2, 1), (1, 1, 2), (1, 1, 1))


def place_of(near, far):
    parity = jnp.bitwise_xor(near, far)
    parity = (parity >> 4 & 1) * 4 + (parity >> 2 & 1) * 2 + (parity & 1)
    extra = [sum(jnp.where(parity == c, step[k], 0) for c, step in enumerate(DETOUR)) for k in range(3)]
    z = ((far >> 4) - (near >> 4) + extra[0]) & 7
    y = ((far >> 2 & 3) - (near >> 2 & 3) + extra[1]) & 3
    x = ((far & 3) - (near & 3) + extra[2]) & 3
    return (parity * 16 + (y >> 1) * 8 + (x >> 1) * 4 + (z >> 1)).astype(jnp.int32)


def cast_kernel(in_ref, out_ref):
    out_ref[...] = in_ref[...].astype(jnp.int8)


def cast_counts(tile_counts):
    tiles, block, _ = tile_counts.shape
    spec = pl.BlockSpec((CHUNK, block, block), lambda i: (i, 0, 0))
    return pl.pallas_call(
        cast_kernel,
        out_shape=jax.ShapeDtypeStruct(tile_counts.shape, jnp.int8),
        grid=(tiles // CHUNK,),
        in_specs=[spec],
        out_specs=spec,
        compiler_params=params(),
        cost_estimate=pl.CostEstimate(flops=tile_counts.size, bytes_accessed=tile_counts.size * 5, transcendentals=0),
        name="cast_counts",
    )(tile_counts)


def for_tiles(far, rounds_ref, work_ref, body):
    start, stop = (rounds_ref[0], rounds_ref[1]) if far else (0, rounds_ref[0])

    def several(step, carry):
        for k in range(UNROLL):
            work = work_ref[step * UNROLL + k]
            body(work & 127, work >> 7 & 255, work >> 15 & 255, work >> 23)
        return carry

    lax.fori_loop(start, stop, several, 0)


def gather_kernel(far, rounds_ref, work_ref, counts_ref, *refs):
    codes = FAR if far else NEAR
    parts, (out_ref, held_ref) = refs[: len(codes)], refs[-2:]
    for code, part in zip(codes, parts):
        held_ref[16 * code : 16 * code + 16] = part[...]
    held_ref[128] = jnp.zeros_like(held_ref[128])
    out_ref[...] = refs[len(codes)][...] if far else jnp.zeros_like(out_ref)

    def body(tile, source, target, slot):
        out_ref[slot] += jnp.dot(counts_ref[tile].astype(f32).astype(bf16), held_ref[source], preferred_element_type=f32)

    for_tiles(far, rounds_ref, work_ref, body)


def gather_products(far, rounds, work, counts, parts, *before):
    tiles, block, _ = counts.shape
    width = parts[0].shape[-1]
    return pl.pallas_call(
        functools.partial(gather_kernel, far),
        out_shape=jax.ShapeDtypeStruct((2, block, width), f32),
        in_specs=[SMEM] * 2 + [VMEM] * (1 + len(parts) + len(before)),
        out_specs=VMEM,
        scratch_shapes=[pltpu.VMEM((129, block, width), bf16)],
        compiler_params=params(),
        cost_estimate=pl.CostEstimate(flops=2 * tiles * block**3, bytes_accessed=counts.size * 2, transcendentals=0),
        name="far_products" if far else "near_products",
    )(rounds, work, counts, *parts, *before)


def dense_kernel(
    scale,
    own_ref,
    other_ref,
    feat_ref,
    feat_other_ref,
    masked_ref,
    masked_other_ref,
    self_ref,
    neigh_ref,
    act_ref,
    back_ref,
    term_ref,
    grad_ref,
):
    contract_last = (((1,), (1,)), ((), ()))
    contract_first = (((0,), (0,)), ((), ()))
    for s, (feat_in, masked_in) in enumerate(((feat_ref, masked_ref), (feat_other_ref, masked_other_ref))):
        feat = feat_in[...]
        neighbour = (scale * (own_ref[s] + other_ref[1 - s])).astype(bf16)
        preact = jnp.dot(feat, self_ref[...], preferred_element_type=f32) + jnp.dot(
            neighbour, neigh_ref[...], preferred_element_type=f32
        )
        sigma = jax.nn.sigmoid(preact)
        delta = (masked_in[...].astype(f32) * sigma * (1.0 + preact * (1.0 - sigma))).astype(bf16)
        back_ref[s] = lax.dot_general(
            neigh_ref[...], delta, contract_last, preferred_element_type=f32
        ).astype(bf16)
        if s == 0:
            act_ref[...] = (preact * sigma).astype(bf16)
            term_ref[...] = lax.dot_general(self_ref[...], delta, contract_last, preferred_element_type=f32)
            for k, value in enumerate((feat, neighbour)):
                grad = lax.dot_general(value, delta, contract_first, preferred_element_type=f32)
                grad_ref[2 * k], grad_ref[2 * k + 1] = grad[:, :128], grad[:, 128:]


def spread_kernel(far, rounds_ref, work_ref, counts_ref, back_ref, *refs):
    codes = FAR if far else NEAR
    outs, held_ref = refs[:-1], refs[-1]
    for code in codes:
        held_ref[16 * code : 16 * code + 16] = jnp.zeros_like(outs[0])
    held_ref[128] = jnp.zeros_like(held_ref[128])

    def body(tile, source, target, slot):
        term = jnp.dot(back_ref[slot], counts_ref[tile].astype(f32).astype(bf16), preferred_element_type=f32).astype(bf16)
        held_ref[target] = (held_ref[target].astype(f32) + term.astype(f32)).astype(bf16)

    for_tiles(far, rounds_ref, work_ref, body)
    for code, out in zip(codes, outs):
        out[...] = held_ref[16 * code : 16 * code + 16]


def spread_terms(far, rounds, work, counts, back):
    tiles, block, _ = counts.shape
    width = back.shape[1]
    outs = len(FAR if far else NEAR)
    return pl.pallas_call(
        functools.partial(spread_kernel, far),
        out_shape=[jax.ShapeDtypeStruct((16, width, block), bf16)] * outs,
        in_specs=[SMEM] * 2 + [VMEM] * 2,
        out_specs=[VMEM] * outs,
        scratch_shapes=[pltpu.VMEM((129, width, block), bf16)],
        compiler_params=params(),
        cost_estimate=pl.CostEstimate(flops=2 * tiles * block**3, bytes_accessed=counts.size * 2, transcendentals=0),
        name="far_terms" if far else "near_terms",
    )(rounds, work, counts, back)


def add_up(refs, index):
    total = refs[0][index].astype(f32)
    for ref in refs[1:]:
        total += ref[index].astype(f32)
    return total


def class_kernel(*refs):
    @pl.loop(0, refs[0].shape[0])
    def _(k):
        refs[-1][k] = add_up(refs[:-1], k).astype(bf16)


def class_sum(parts):
    return pl.pallas_call(
        class_kernel,
        out_shape=jax.ShapeDtypeStruct(parts[0].shape, bf16),
        in_specs=[VMEM] * len(parts),
        out_specs=VMEM,
        compiler_params=params(),
        name="class_sum",
    )(*parts)


def joint_kernel(cells_ref, *refs):
    ins, outs = refs[:5], refs[5:]
    rows = ins[0].shape[1]
    for k, out in enumerate(outs):
        for z in range(4):
            out[z * rows : z * rows + rows] = add_up(ins, 4 * k + z).astype(bf16)
        out[4 * rows :] = cells_ref[...].astype(bf16)


def joint_sum(cells, parts):
    _, rows, columns = parts[0].shape
    return pl.pallas_call(
        joint_kernel,
        out_shape=[jax.ShapeDtypeStruct((4 * rows + cells.shape[0], columns), bf16)] * 4,
        in_specs=[VMEM] * 6,
        out_specs=[VMEM] * 4,
        compiler_params=params(),
        name="joint_sum",
    )(cells, *parts)


def plane_kernel(*refs):
    ins, outs = refs[:4], refs[4:]
    rows = 128
    for z, out in enumerate(outs):
        out[:rows] = add_up(ins, slice(z * rows, z * rows + rows)).astype(bf16)
        for k, part in enumerate(ins):
            out[rows + 32 * k : rows + 32 * k + 32] = part[4 * rows :]


def plane_sum(parts):
    columns = parts[0].shape[1]
    return pl.pallas_call(
        plane_kernel,
        out_shape=[jax.ShapeDtypeStruct((256, columns), bf16)] * 4,
        in_specs=[VMEM] * 4,
        out_specs=[VMEM] * 4,
        compiler_params=params(),
        name="plane_sum",
    )(*parts)


def last_kernel(scale, grad_scale, order_ref, *refs):
    ins, (term_ref, out_ref, self_ref, neigh_ref, cells_ref) = refs[:4], refs[4:]
    rows = term_ref.shape[0]
    total = add_up(ins, slice(0, rows))
    out_ref[...] = (term_ref[...] + scale * total).T
    for z, part in enumerate(ins):
        for k in range(4):
            cells = part[rows + 32 * k : rows + 32 * k + 32].astype(f32)
            cells_ref[order_ref[4 * k + z]] = grad_scale * cells
    for k in range(16):
        ref = (self_ref, neigh_ref)[k // 8]
        ref[k % 4 * 32 : k % 4 * 32 + 32, k // 4 % 2 * 128 : k // 4 % 2 * 128 + 128] = cells_ref[k]


def gather_blocks(features, tile_counts, *ready):
    own = features[None]
    own = jnp.concatenate([own, move(own, 2, 0, 0), move(own, 4, 0, 0), move(own, -2, 0, 0)])
    own = jnp.concatenate([own, move(own, 0, 0, 2), move(own, 0, 2, 0), move(own, 0, 2, 2)])
    own, tile_counts = lax.optimization_barrier((own, tile_counts))
    far = move(own, -1, -1, -1)
    counts = cast_counts(tile_counts)
    far, counts, *ready = lax.optimization_barrier((far, counts, *ready))
    near = [own, move(own, 0, 0, 1), move(own, 0, 1, 0), move(own, 1, 0, 0), far]
    return near, [move(far, -1, 0, 0), move(far, 0, -1, 0), move(far, 0, 0, -1)], counts, *ready


def shards(
    features, tile_counts, tile_row, tile_col, label_ids, cotangent, self_weight, neigh_weight
):
    half_rows, width_in = features.shape
    hidden = cotangent.shape[1]
    tile_total, block, _ = tile_counts.shape
    reps, devices = lax.axis_size("rep"), lax.axis_size(ALL)
    rep = lax.axis_index("rep")
    scale = (edge_moment * tile_total * reps * block / 2) ** (-0.5)
    swap = [(0, 1), (1, 0)]

    owner, here = tile_col >> 1, lax.axis_index(ROWS)
    source, target = place_of(owner, here), place_of(here, owner)
    step = jnp.arange(16, dtype=jnp.int32)
    order = ((here >> 5) - step & 3) * 4 + ((here >> 3) + (step >> 3) & 1) * 2 + ((here >> 1) + (step >> 2) & 1)
    slot = jnp.bitwise_xor(tile_row, rep)
    tiles = jnp.arange(tile_total, dtype=jnp.int32)
    near_tile = functools.reduce(jnp.logical_and, [source // 16 != code for code in FAR])
    before = tiles[None, :] < tiles[:, None]
    rank = jnp.sum(before & (near_tile[None, :] == near_tile[:, None]), axis=1, dtype=jnp.int32)
    near_rounds = jnp.sum(near_tile, dtype=jnp.int32) + UNROLL - 1 >> 3
    far_rounds = jnp.sum(~near_tile, dtype=jnp.int32) + UNROLL - 1 >> 3
    rounds = jnp.stack([near_rounds, near_rounds + far_rounds])
    rank = jnp.where(near_tile, rank, near_rounds * UNROLL + rank)
    unused = 128 * 2**7 + 128 * 2**15
    work = tiles + source * 2**7 + target * 2**15 + slot * 2**23 - unused
    entries = jnp.arange(tile_total + 2 * UNROLL, dtype=jnp.int32)
    work = unused + jnp.sum(jnp.where(rank[None, :] == entries[:, None], work[None, :], 0), axis=1, dtype=jnp.int32)

    local_ids = label_ids % half_rows
    label_mask = jnp.any(local_ids[:, None] == jnp.arange(half_rows, dtype=jnp.int32)[None, :], axis=0)
    masked = jnp.where(label_mask[:, None], cotangent, jnp.zeros_like(cotangent))
    near, far, counts, rounds, work, masked = gather_blocks(features, tile_counts, rounds, work, masked)
    features_other = lax.ppermute(features, "rep", swap)
    masked_other = lax.ppermute(masked, "rep", swap)

    own = gather_products(False, rounds, work, counts, near)
    own, features_other, masked_other = lax.optimization_barrier((own, features_other, masked_other))
    own = gather_products(True, rounds, work, counts, far, own)
    other = lax.ppermute(own, "rep", swap)

    activation, back, own_term, grads = pl.pallas_call(
        functools.partial(dense_kernel, scale),
        out_shape=(
            jax.ShapeDtypeStruct((half_rows, hidden), bf16),
            jax.ShapeDtypeStruct((2, width_in, half_rows), bf16),
            jax.ShapeDtypeStruct((width_in, half_rows), f32),
            jax.ShapeDtypeStruct((4, width_in, 128), f32),
        ),
        compiler_params=params(),
        name="dense",
    )(own, other, features, features_other, masked, masked_other, self_weight, neigh_weight)

    grads_other = lax.ppermute(grads, "rep", swap)
    far = spread_terms(True, rounds, work, counts, back)
    grads = grads + grads_other
    far = [move(far[0], -1, 0, 0), move(far[1], 0, -1, 0), move(far[2], 0, 0, -1)]
    near = spread_terms(False, rounds, work, counts, back)
    *near, grads = lax.optimization_barrier((*near, grads))
    parts = [near[0], move(near[1], 0, 0, 1), move(near[2], 0, 1, 0), move(near[3], 1, 0, 0)]
    parts.append(move(class_sum([near[4], *far]), -1, -1, -1))

    cells = grads.reshape(lax.axis_size(HIGH), -1, 128)
    cells = jnp.sum(lax.all_to_all(cells, HIGH, 0, 0, tiled=True), axis=0)
    cells = jnp.sum(spread(cells, LOW), axis=0)
    parts = joint_sum(cells, parts)
    parts = plane_sum([parts[0], move(parts[1], 0, 0, 2), move(parts[2], 0, 2, 0), move(parts[3], 0, 2, 2)])
    parts = [parts[0], move(parts[1], 2, 0, 0), move(parts[2], 4, 0, 0), move(parts[3], -2, 0, 0)]
    grad_scale = float(label_ids.shape[0] * devices) ** (-0.5)
    grad_shape = jax.ShapeDtypeStruct((width_in, hidden), f32)
    grad_features, grad_self, grad_neigh = pl.pallas_call(
        functools.partial(last_kernel, scale, grad_scale),
        out_shape=(jax.ShapeDtypeStruct((half_rows, width_in), f32), grad_shape, grad_shape),
        in_specs=[SMEM] + [VMEM] * 5,
        out_specs=(VMEM, VMEM, VMEM),
        scratch_shapes=[pltpu.VMEM((16, 32, 128), f32)],
        compiler_params=params(),
        name="last_sum",
    )(order, *parts, own_term)
    return activation, grad_features, grad_self, grad_neigh


def solution(mesh):
    grid = Mesh(mesh.devices.reshape(4, 2, 2, 2, 2, 2, 2), ALL)
    placed = (
        P(ALL, None),
        P(ALL, None, None),
        P(ALL),
        P(ALL),
        P(ALL),
        P(ALL, None),
        P(),
        P(),
    )
    return jax.shard_map(
        shards,
        mesh=grid,
        in_specs=placed,
        out_specs=(P(ALL, None), P(ALL, None), P(), P()),
        check_vma=False,
    )
```

```python
import functools

import jax
import jax.numpy as jnp
from jax import lax
from jax.experimental import pallas as pl
from jax.experimental.pallas import tpu as pltpu
from jax.sharding import Mesh
from jax.sharding import PartitionSpec as P

edge_moment = 14.0 / 96.0
f32, bf16 = jnp.float32, jnp.bfloat16
CHUNK = 16
UNROLL = 8
NEAR, FAR = (0, 1, 2, 4, 7), (3, 5, 6)
HIGH, LOW = ("zq", "yq", "xq"), ("zp", "yp", "xp")
ROWS = ("zq", "zp", "yq", "yp", "xq", "xp")
ALL = ROWS + ("rep",)
VMEM_LIMIT = 16 * 2**20
SMEM = pl.BlockSpec(memory_space=pltpu.SMEM)
VMEM = pl.BlockSpec(memory_space=pltpu.VMEM)
def params():
    return pltpu.CompilerParams(vmem_limit_bytes=VMEM_LIMIT)


def whole(shape):
    return pl.BlockSpec(shape, lambda *_: (0,) * len(shape))


def move(block, dz, dy, dx):
    pairs = [
        (z * 16 + y * 4 + x, (z + dz) % 8 * 16 + (y + dy) % 4 * 4 + (x + dx) % 4)
        for z in range(8)
        for y in range(4)
        for x in range(4)
    ]
    return lax.ppermute(block, ROWS, pairs)


def spread(block, axes):
    count = 1
    for axis in axes:
        count *= lax.axis_size(axis)
    copies = jnp.broadcast_to(block[None], (count,) + block.shape)
    return lax.all_to_all(copies, axes, 0, 0, tiled=True)


DETOUR = ((0, 0, 0), (0, 0, -1), (0, -1, 0), (2, 1, 1), (-1, 0, 0), (1, 2, 1), (1, 1, 2), (1, 1, 1))


def place_of(near, far):
    parity = jnp.bitwise_xor(near, far)
    parity = (parity >> 4 & 1) * 4 + (parity >> 2 & 1) * 2 + (parity & 1)
    extra = [sum(jnp.where(parity == c, step[k], 0) for c, step in enumerate(DETOUR)) for k in range(3)]
    z = ((far >> 4) - (near >> 4) + extra[0]) & 7
    y = ((far >> 2 & 3) - (near >> 2 & 3) + extra[1]) & 3
    x = ((far & 3) - (near & 3) + extra[2]) & 3
    return (parity * 16 + (y >> 1) * 8 + (x >> 1) * 4 + (z >> 1)).astype(jnp.int32)


def cast_kernel(in_ref, out_ref):
    out_ref[...] = in_ref[...].astype(jnp.int8)


def cast_counts(tile_counts):
    tiles, block, _ = tile_counts.shape
    spec = pl.BlockSpec((CHUNK, block, block), lambda i: (i, 0, 0))
    return pl.pallas_call(
        cast_kernel,
        out_shape=jax.ShapeDtypeStruct(tile_counts.shape, jnp.int8),
        grid=(tiles // CHUNK,),
        in_specs=[spec],
        out_specs=spec,
        compiler_params=params(),
        cost_estimate=pl.CostEstimate(flops=tile_counts.size, bytes_accessed=tile_counts.size * 5, transcendentals=0),
        name="cast_counts",
    )(tile_counts)


def for_tiles(far, rounds_ref, work_ref, body):
    start, stop = (rounds_ref[0], rounds_ref[1]) if far else (0, rounds_ref[0])

    def several(step, carry):
        for k in range(UNROLL):
            work = work_ref[step * UNROLL + k]
            body(work & 127, work >> 7 & 255, work >> 15 & 255, work >> 23)
        return carry

    lax.fori_loop(start, stop, several, 0)


def gather_kernel(far, rounds_ref, work_ref, counts_ref, *refs):
    codes = FAR if far else NEAR
    parts, (out_ref, held_ref) = refs[: len(codes)], refs[-2:]
    for code, part in zip(codes, parts):
        held_ref[16 * code : 16 * code + 16] = part[...]
    held_ref[128] = jnp.zeros_like(held_ref[128])
    out_ref[...] = refs[len(codes)][...] if far else jnp.zeros_like(out_ref)

    def body(tile, source, target, slot):
        out_ref[slot] += jnp.dot(counts_ref[tile].astype(f32).astype(bf16), held_ref[source], preferred_element_type=f32)

    for_tiles(far, rounds_ref, work_ref, body)


def gather_products(far, rounds, work, counts, parts, *before):
    tiles, block, _ = counts.shape
    width = parts[0].shape[-1]
    return pl.pallas_call(
        functools.partial(gather_kernel, far),
        out_shape=jax.ShapeDtypeStruct((2, block, width), f32),
        in_specs=[SMEM] * 2 + [VMEM] * (1 + len(parts) + len(before)),
        out_specs=VMEM,
        scratch_shapes=[pltpu.VMEM((129, block, width), bf16)],
        compiler_params=params(),
        cost_estimate=pl.CostEstimate(flops=2 * tiles * block**3, bytes_accessed=counts.size * 2, transcendentals=0),
        name="far_products" if far else "near_products",
    )(rounds, work, counts, *parts, *before)


def dense_kernel(
    scale,
    own_ref,
    other_ref,
    feat_ref,
    feat_other_ref,
    masked_ref,
    masked_other_ref,
    self_ref,
    neigh_ref,
    act_ref,
    back_ref,
    term_ref,
    grad_ref,
):
    contract_last = (((1,), (1,)), ((), ()))
    contract_first = (((0,), (0,)), ((), ()))
    for s, (feat_in, masked_in) in enumerate(((feat_ref, masked_ref), (feat_other_ref, masked_other_ref))):
        feat = feat_in[...]
        neighbour = (scale * (own_ref[s] + other_ref[1 - s])).astype(bf16)
        preact = jnp.dot(feat, self_ref[...], preferred_element_type=f32) + jnp.dot(
            neighbour, neigh_ref[...], preferred_element_type=f32
        )
        sigma = jax.nn.sigmoid(preact)
        delta = (masked_in[...].astype(f32) * sigma * (1.0 + preact * (1.0 - sigma))).astype(bf16)
        back_ref[s] = lax.dot_general(
            neigh_ref[...], delta, contract_last, preferred_element_type=f32
        ).astype(bf16)
        if s == 0:
            act_ref[...] = (preact * sigma).astype(bf16)
            term_ref[...] = lax.dot_general(self_ref[...], delta, contract_last, preferred_element_type=f32)
            for k, value in enumerate((feat, neighbour)):
                grad = lax.dot_general(value, delta, contract_first, preferred_element_type=f32)
                grad_ref[2 * k], grad_ref[2 * k + 1] = grad[:, :128], grad[:, 128:]


def spread_kernel(far, rounds_ref, work_ref, counts_ref, back_ref, *refs):
    codes = FAR if far else NEAR
    outs, held_ref = refs[:-1], refs[-1]
    for code in codes:
        held_ref[16 * code : 16 * code + 16] = jnp.zeros_like(outs[0])
    held_ref[128] = jnp.zeros_like(held_ref[128])

    def body(tile, source, target, slot):
        term = jnp.dot(back_ref[slot], counts_ref[tile].astype(f32).astype(bf16), preferred_element_type=f32).astype(bf16)
        held_ref[target] = (held_ref[target].astype(f32) + term.astype(f32)).astype(bf16)

    for_tiles(far, rounds_ref, work_ref, body)
    for code, out in zip(codes, outs):
        out[...] = held_ref[16 * code : 16 * code + 16]


def spread_terms(far, rounds, work, counts, back):
    tiles, block, _ = counts.shape
    width = back.shape[1]
    outs = len(FAR if far else NEAR)
    return pl.pallas_call(
        functools.partial(spread_kernel, far),
        out_shape=[jax.ShapeDtypeStruct((16, width, block), bf16)] * outs,
        in_specs=[SMEM] * 2 + [VMEM] * 2,
        out_specs=[VMEM] * outs,
        scratch_shapes=[pltpu.VMEM((129, width, block), bf16)],
        compiler_params=params(),
        cost_estimate=pl.CostEstimate(flops=2 * tiles * block**3, bytes_accessed=counts.size * 2, transcendentals=0),
        name="far_terms" if far else "near_terms",
    )(rounds, work, counts, back)


def add_up(refs, index):
    total = refs[0][index].astype(f32)
    for ref in refs[1:]:
        total += ref[index].astype(f32)
    return total


def class_kernel(*refs):
    for k in range(refs[0].shape[0]):
        refs[-1][k] = add_up(refs[:-1], k).astype(bf16)


def class_sum(parts):
    count, rows, columns = parts[0].shape
    spec = pl.BlockSpec((count // 4, rows, columns), lambda i: (i, 0, 0))
    return pl.pallas_call(
        class_kernel,
        out_shape=jax.ShapeDtypeStruct(parts[0].shape, bf16),
        grid=(4,),
        in_specs=[spec] * len(parts),
        out_specs=spec,
        compiler_params=params(),
        name="class_sum",
    )(*parts)


def joint_kernel(cells_ref, *refs):
    ins, outs = refs[:5], refs[5:]
    rows = ins[0].shape[1]
    for k, out in enumerate(outs):
        for z in range(4):
            out[z * rows : z * rows + rows] = add_up(ins, 4 * k + z).astype(bf16)
        out[4 * rows :] = cells_ref[...].astype(bf16)


def joint_sum(cells, parts):
    _, rows, columns = parts[0].shape
    return pl.pallas_call(
        joint_kernel,
        out_shape=[jax.ShapeDtypeStruct((4 * rows + cells.shape[0], columns), bf16)] * 4,
        in_specs=[VMEM] * 6,
        out_specs=[VMEM] * 4,
        compiler_params=params(),
        name="joint_sum",
    )(cells, *parts)


def plane_kernel(*refs):
    ins, outs = refs[:4], refs[4:]
    rows = 128
    for z, out in enumerate(outs):
        out[:rows] = add_up(ins, slice(z * rows, z * rows + rows)).astype(bf16)
        for k, part in enumerate(ins):
            out[rows + 32 * k : rows + 32 * k + 32] = part[4 * rows :]


def plane_sum(parts):
    columns = parts[0].shape[1]
    return pl.pallas_call(
        plane_kernel,
        out_shape=[jax.ShapeDtypeStruct((256, columns), bf16)] * 4,
        in_specs=[VMEM] * 4,
        out_specs=[VMEM] * 4,
        compiler_params=params(),
        name="plane_sum",
    )(*parts)


def last_kernel(scale, grad_scale, order_ref, *refs):
    ins, (term_ref, out_ref, self_ref, neigh_ref, cells_ref) = refs[:4], refs[4:]
    rows = term_ref.shape[0]
    total = add_up(ins, slice(0, rows))
    out_ref[...] = (term_ref[...] + scale * total).T
    for z, part in enumerate(ins):
        for k in range(4):
            cells = part[rows + 32 * k : rows + 32 * k + 32].astype(f32)
            cells_ref[order_ref[4 * k + z]] = grad_scale * cells
    for k in range(16):
        ref = (self_ref, neigh_ref)[k // 8]
        ref[k % 4 * 32 : k % 4 * 32 + 32, k // 4 % 2 * 128 : k // 4 % 2 * 128 + 128] = cells_ref[k]


def gather_blocks(features, tile_counts, *ready):
    own = features[None]
    own = jnp.concatenate([own, move(own, 2, 0, 0), move(own, 4, 0, 0), move(own, -2, 0, 0)])
    own = jnp.concatenate([own, move(own, 0, 0, 2), move(own, 0, 2, 0), move(own, 0, 2, 2)])
    own, tile_counts = lax.optimization_barrier((own, tile_counts))
    far = move(own, -1, -1, -1)
    counts = cast_counts(tile_counts)
    far, counts, *ready = lax.optimization_barrier((far, counts, *ready))
    near = [own, move(own, 0, 0, 1), move(own, 0, 1, 0), move(own, 1, 0, 0), far]
    return near, [move(far, -1, 0, 0), move(far, 0, -1, 0), move(far, 0, 0, -1)], counts, *ready


def shards(
    features, tile_counts, tile_row, tile_col, label_ids, cotangent, self_weight, neigh_weight
):
    half_rows, width_in = features.shape
    hidden = cotangent.shape[1]
    tile_total, block, _ = tile_counts.shape
    reps, devices = lax.axis_size("rep"), lax.axis_size(ALL)
    rep = lax.axis_index("rep")
    scale = (edge_moment * tile_total * reps * block / 2) ** (-0.5)
    swap = [(0, 1), (1, 0)]

    owner, here = tile_col >> 1, lax.axis_index(ROWS)
    source, target = place_of(owner, here), place_of(here, owner)
    step = jnp.arange(16, dtype=jnp.int32)
    order = ((here >> 5) - step & 3) * 4 + ((here >> 3) + (step >> 3) & 1) * 2 + ((here >> 1) + (step >> 2) & 1)
    slot = jnp.bitwise_xor(tile_row, rep)
    tiles = jnp.arange(tile_total, dtype=jnp.int32)
    near_tile = functools.reduce(jnp.logical_and, [source // 16 != code for code in FAR])
    before = tiles[None, :] < tiles[:, None]
    rank = jnp.sum(before & (near_tile[None, :] == near_tile[:, None]), axis=1, dtype=jnp.int32)
    near_rounds = jnp.sum(near_tile, dtype=jnp.int32) + UNROLL - 1 >> 3
    far_rounds = jnp.sum(~near_tile, dtype=jnp.int32) + UNROLL - 1 >> 3
    rounds = jnp.stack([near_rounds, near_rounds + far_rounds])
    rank = jnp.where(near_tile, rank, near_rounds * UNROLL + rank)
    unused = 128 * 2**7 + 128 * 2**15
    work = tiles + source * 2**7 + target * 2**15 + slot * 2**23 - unused
    entries = jnp.arange(tile_total + 2 * UNROLL, dtype=jnp.int32)
    work = unused + jnp.sum(jnp.where(rank[None, :] == entries[:, None], work[None, :], 0), axis=1, dtype=jnp.int32)

    local_ids = label_ids % half_rows
    label_mask = jnp.any(local_ids[:, None] == jnp.arange(half_rows, dtype=jnp.int32)[None, :], axis=0)
    masked = jnp.where(label_mask[:, None], cotangent, jnp.zeros_like(cotangent))
    near, far, counts, rounds, work, masked = gather_blocks(features, tile_counts, rounds, work, masked)
    features_other = lax.ppermute(features, "rep", swap)
    masked_other = lax.ppermute(masked, "rep", swap)

    own = gather_products(False, rounds, work, counts, near)
    own, features_other, masked_other = lax.optimization_barrier((own, features_other, masked_other))
    own = gather_products(True, rounds, work, counts, far, own)
    other = lax.ppermute(own, "rep", swap)

    activation, back, own_term, grads = pl.pallas_call(
        functools.partial(dense_kernel, scale),
        out_shape=(
            jax.ShapeDtypeStruct((half_rows, hidden), bf16),
            jax.ShapeDtypeStruct((2, width_in, half_rows), bf16),
            jax.ShapeDtypeStruct((width_in, half_rows), f32),
            jax.ShapeDtypeStruct((4, width_in, 128), f32),
        ),
        compiler_params=params(),
        name="dense",
    )(own, other, features, features_other, masked, masked_other, self_weight, neigh_weight)

    grads_other = lax.ppermute(grads, "rep", swap)
    far = spread_terms(True, rounds, work, counts, back)
    grads = grads + grads_other
    far = [move(far[0], -1, 0, 0), move(far[1], 0, -1, 0), move(far[2], 0, 0, -1)]
    near = spread_terms(False, rounds, work, counts, back)
    *near, grads = lax.optimization_barrier((*near, grads))
    parts = [near[0], move(near[1], 0, 0, 1), move(near[2], 0, 1, 0), move(near[3], 1, 0, 0)]
    parts.append(move(class_sum([near[4], *far]), -1, -1, -1))

    cells = grads.reshape(lax.axis_size(HIGH), -1, 128)
    cells = jnp.sum(lax.all_to_all(cells, HIGH, 0, 0, tiled=True), axis=0)
    cells = jnp.sum(spread(cells, LOW), axis=0)
    parts = joint_sum(cells, parts)
    parts = plane_sum([parts[0], move(parts[1], 0, 0, 2), move(parts[2], 0, 2, 0), move(parts[3], 0, 2, 2)])
    parts = [parts[0], move(parts[1], 2, 0, 0), move(parts[2], 4, 0, 0), move(parts[3], -2, 0, 0)]
    grad_scale = float(label_ids.shape[0] * devices) ** (-0.5)
    grad_shape = jax.ShapeDtypeStruct((width_in, hidden), f32)
    grad_features, grad_self, grad_neigh = pl.pallas_call(
        functools.partial(last_kernel, scale, grad_scale),
        out_shape=(jax.ShapeDtypeStruct((half_rows, width_in), f32), grad_shape, grad_shape),
        in_specs=[SMEM] + [VMEM] * 5,
        out_specs=(VMEM, VMEM, VMEM),
        scratch_shapes=[pltpu.VMEM((16, 32, 128), f32)],
        compiler_params=params(),
        name="last_sum",
    )(order, *parts, own_term)
    return activation, grad_features, grad_self, grad_neigh


def solution(mesh):
    grid = Mesh(mesh.devices.reshape(4, 2, 2, 2, 2, 2, 2), ALL)
    placed = (
        P(ALL, None),
        P(ALL, None, None),
        P(ALL),
        P(ALL),
        P(ALL),
        P(ALL, None),
        P(),
        P(),
    )
    return jax.shard_map(
        shards,
        mesh=grid,
        in_specs=placed,
        out_specs=(P(ALL, None), P(ALL, None), P(), P()),
        check_vma=False,
    )
```
